32 devices in a mesh: lat: 4 (over y, x), lon: 8 (over z, core).
Axes of the slice: x: 2, y: 2, z: 4, core: 2. Of those that a mesh axis runs over, the one named last changes fastest.
Arguments:
- features: bfloat16 [128, 1024, 128], P('lat', 'lon'), may hold values from -6 to 6
- land_mask: int32 [128, 1024], P('lat', 'lon'), may hold values 0 or 1
- dw_weight: float32 [7, 7, 128], replicated, may hold values from -0.875 to 0.875
- dw_bias: float32 [128], replicated, may hold values from -3 to 3
- norm_gain: float32 [128], replicated, may hold values from 0.25 to 1.75
- norm_shift: float32 [128], replicated, may hold values from -3 to 3
- expand_weight: bfloat16 [128, 512], replicated, may hold values from -0.5 to 0.5
- expand_bias: float32 [512], replicated, may hold values from -3 to 3
- project_weight: bfloat16 [512, 128], replicated, may hold values from -0.25 to 0.25
- project_bias: float32 [128], replicated, may hold values from -3 to 3
- layer_scale: float32 [128], replicated, may hold values from 0.3 to 1
- out_gain: float32 [128], replicated, may hold values from 0.25 to 1.75
- out_shift: float32 [128], replicated, may hold values from -3 to 3
- coarse_weight: bfloat16 [4, 4, 128, 256], replicated, may hold values from -0.125 to 0.125
- coarse_bias: float32 [256], replicated, may hold values from -3 to 3
Outputs:
- coarse: bfloat16 [64, 512, 256], P('lat', 'lon')
The draws below stay inside these ranges and needn't reach their ends.
All inputs are finite; a program needn't handle non-finite values. No bound on the sum of `land_mask` on one device may be relied on, other than what follows from the above.
Results may differ from the reference program's by a relative error of at most 0.0051.
Values may be sent and summed in bfloat16 or wider, within the bound.
A program may use at most 64 MiB of HBM per device.

```python
import math
import jax
import jax.numpy as jnp
from jax import lax

C = 128
HID = 512
OUT = 256
KS = 7
CY = 32
NY = 128
NX = 1024
N_LAT = 4


def set_ends(drawn, own_key, smallest, top_value):
    dims = drawn.shape
    place = [jax.random.randint(jax.random.fold_in(own_key, axis), (), 0, dims[axis]) for axis in range(len(dims))]
    drawn = drawn.at[tuple(place)].set(smallest)
    longest = dims.index(max(dims))
    place[longest] = (place[longest] + 1) % dims[longest]
    return drawn.at[tuple(place)].set(top_value)


def steps_of(rng, dims, split, smallest, top_value):
    level = 1.0
    for position, shards_of in split:
        heights = jax.random.uniform(jax.random.fold_in(jax.random.fold_in(rng, 6), position), (shards_of,), jnp.float32, smallest / len(split), top_value / len(split))
        level = level * jnp.repeat(jnp.exp(heights), dims[position] // shards_of).reshape((-1,) + (1,) * (len(dims) - 1 - position))
    return level


def gaussian(own_key, extent, scale, limit, shards=(), held_as=jnp.bfloat16):
    array = jax.random.normal(own_key, extent, jnp.float32) * scale
    if len(shards) > 0:
        array = steps_of(own_key, extent, shards, -0.22, 0.18) * array
    return jnp.clip(array, min=-limit, max=limit).astype(held_as)


def setup_inputs(seed: int = 0) -> dict:
    key_list = jax.random.split(jax.random.key(seed), 16)
    return {
        "features": gaussian(key_list[0], (NY, NX, C), 1.0, 6.0, ((0, 4), (1, 8))),
        "land_mask": set_ends((jax.random.randint(key_list[1], (NY, NX), 0, 4) < 3).astype(jnp.int32), jax.random.fold_in(key_list[1], 1), 0, 1),
        "dw_weight": gaussian(key_list[2], (KS, KS, C), (KS * KS) ** -0.5, 0.875, (), jnp.float32),
        "dw_bias": gaussian(key_list[3], (C,), 0.5, 3.0, (), jnp.float32),
        "norm_gain": jnp.clip(1.0 + 0.15 * jax.random.normal(key_list[4], (C,), jnp.float32), 0.25, 1.75),
        "norm_shift": gaussian(key_list[5], (C,), 0.5, 3.0, (), jnp.float32),
        "expand_weight": gaussian(key_list[6], (C, HID), C ** -0.5, 0.5),
        "expand_bias": gaussian(key_list[7], (HID,), 0.5, 3.0, (), jnp.float32),
        "project_weight": gaussian(key_list[8], (HID, C), HID ** -0.5, 0.25),
        "project_bias": gaussian(key_list[9], (C,), 0.5, 3.0, (), jnp.float32),
        "layer_scale": jnp.clip(jnp.exp(jax.random.uniform(key_list[10], (C,), jnp.float32, math.log(0.3), math.log(1.0))), 0.3, 1.0),
        "out_gain": jnp.clip(1.0 + 0.15 * jax.random.normal(key_list[11], (C,), jnp.float32), 0.25, 1.75),
        "out_shift": gaussian(key_list[12], (C,), 0.5, 3.0, (), jnp.float32),
        "coarse_weight": gaussian(key_list[13], (4, 4, C, OUT), (16 * C) ** -0.5, 0.125),
        "coarse_bias": gaussian(key_list[14], (OUT,), 0.5, 3.0, (), jnp.float32),
    }


def layer_norm(values, gain, shift):
    center = values - lax.optimization_barrier(jnp.mean(values, axis=-1, keepdims=True))
    spread = lax.optimization_barrier(jnp.mean(center * center, axis=-1, keepdims=True))
    return center * lax.rsqrt(spread + 1e-06) * gain + shift

def extend_global(grid_field, rim_size):
    widened = jnp.concatenate([grid_field[:, -rim_size:], grid_field, grid_field[:, :rim_size]], axis=1)
    north_rim = widened[-rim_size:][::-1, ::-1]
    south_rim = jnp.zeros_like(widened[:rim_size])
    return jnp.concatenate([south_rim, widened, north_rim], axis=0)

def convnext_cells(padded_in, centre, land_mask, dw_weight, dw_bias, norm_gain, norm_shift, expand_weight, expand_bias, project_weight, project_bias, layer_scale, out_gain, out_shift):
    height, breadth, channels = centre.shape
    spatial = jnp.zeros(centre.shape, jnp.float32) + dw_bias
    for row_tap in range(dw_weight.shape[0]):
        for col_tap in range(dw_weight.shape[1]):
            spatial = spatial + padded_in[row_tap:row_tap + height, col_tap:col_tap + breadth].astype(jnp.float32) * dw_weight[row_tap, col_tap]
    normed = layer_norm(spatial, norm_gain, norm_shift).astype(jnp.bfloat16).reshape(-1, channels)
    hidden = jax.nn.gelu(jnp.dot(normed, expand_weight, preferred_element_type=jnp.float32) + expand_bias, approximate=False).astype(jnp.bfloat16)
    updated = centre.reshape(-1, channels).astype(jnp.float32) + layer_scale * (jnp.dot(hidden, project_weight, preferred_element_type=jnp.float32) + project_bias)
    marks = land_mask.reshape(-1, 1).astype(jnp.float32)
    normalized = marks * layer_norm(updated, out_gain, out_shift)
    return normalized.astype(jnp.bfloat16).reshape(height, breadth, channels)

def shrink_cells(padded, coarse_weight, coarse_bias):
    height = padded.shape[0] - 2
    breadth = padded.shape[1] - 2
    channels = padded.shape[2]
    total = jnp.zeros((height // 2 * (breadth // 2), coarse_weight.shape[3]), jnp.float32) + coarse_bias
    for row_tap in range(4):
        for col_tap in range(4):
            window = padded[row_tap:row_tap + height:2, col_tap:col_tap + breadth:2].reshape(-1, channels)
            total = total + jnp.dot(window, coarse_weight[row_tap, col_tap], preferred_element_type=jnp.float32)
    return total.astype(jnp.bfloat16).reshape(height // 2, breadth // 2, coarse_weight.shape[3])

def reference(features, land_mask, dw_weight, dw_bias, norm_gain, norm_shift, expand_weight, expand_bias, project_weight, project_bias, layer_scale, out_gain, out_shift, coarse_weight, coarse_bias):
    padded_in = extend_global(features, 3)

    def block_rows(block_index):
        offset = (block_index * CY).astype(jnp.int32)
        rows_in = lax.dynamic_slice_in_dim(padded_in, offset, CY + 6, 0)
        centre = lax.dynamic_slice_in_dim(features, offset, CY, 0)
        marks = lax.dynamic_slice_in_dim(land_mask, offset, CY, 0)
        return convnext_cells(rows_in, centre, marks, dw_weight, dw_bias, norm_gain, norm_shift, expand_weight, expand_bias, project_weight, project_bias, layer_scale, out_gain, out_shift)
    normalized = lax.map(block_rows, jnp.arange(N_LAT, dtype=jnp.int32)).reshape(NY, NX, C)
    padded_out = extend_global(normalized, 1)

    def coarse_rows(block_index):
        offset = (block_index * CY).astype(jnp.int32)
        rows_in = lax.dynamic_slice_in_dim(padded_out, offset, CY + 2, 0)
        return shrink_cells(rows_in, coarse_weight, coarse_bias)
    coarse = lax.map(coarse_rows, jnp.arange(N_LAT, dtype=jnp.int32))
    return coarse.reshape(NY // 2, NX // 2, OUT)
```

```python
import functools

import jax
import jax.numpy as jnp
from jax import lax
from jax.experimental import pallas as pl
from jax.experimental.pallas import tpu as pltpu
from jax.sharding import PartitionSpec as P

MESH = pl.DeviceIdType.MESH
F32 = jnp.float32
BF16 = jnp.bfloat16
FAR = 8
EDGE = 16


def gelu(values):
    return 0.5 * values * (1.0 + lax.erf(values * 0.7071067811865476))


def layer_norm(values, gain, shift):
    center = values - jnp.mean(values, axis=-1, keepdims=True)
    spread = jnp.mean(center * center, axis=-1, keepdims=True)
    return center * lax.rsqrt(spread + 1e-06) * gain + shift


def body(
    feat,
    mask,
    dw,
    dw_bias,
    gain1,
    shift1,
    w1,
    b1,
    w2,
    b2,
    scale,
    gain2,
    shift2,
    cw_hbm,
    cb,
    out,
    slab,
    rows,
    corners,
    wide,
    ghost_wide,
    ext,
    taps,
    conv_out,
    nrm,
    side_out,
    side_in,
    stage,
    cw,
    coarse,
    slab_send,
    slab_recv,
    rows_send,
    rows_recv,
    corner_send,
    corner_recv,
    side_send,
    side_recv,
    stage_send,
    stage_recv,
    cw_sem,
):
    height, breadth, ch = feat.shape
    ks = dw.shape[0]
    rim = ks // 2
    blocks = breadth // FAR
    n_off = FAR + 2 * rim
    units = height // 4
    lat, lon = lax.axis_index("lat"), lax.axis_index("lon")
    n_lat, n_lon = lax.axis_size("lat"), lax.axis_size("lon")
    top = lat == n_lat - 1
    east, west = lax.rem(lon + 1, n_lon), lax.rem(lon + n_lon - 1, n_lon)
    north_lat = jnp.where(top, lat, lat + 1)
    north_lon = jnp.where(top, n_lon - 1 - lon, lon)
    north = (north_lat, north_lon)
    north_slot = jnp.where(top, 1, 0)
    south = (jnp.maximum(lat - 1, 0), lon)

    load_cw = pltpu.make_async_copy(cw_hbm, cw, cw_sem)
    load_cw.start()

    barrier = pltpu.get_barrier_semaphore()
    for target in ((lat, east), (lat, west), north):
        pl.semaphore_signal(barrier, inc=1, device_id=target, device_id_type=MESH)

    @pl.when(lat > 0)
    def _():
        pl.semaphore_signal(barrier, inc=1, device_id=south, device_id_type=MESH)

    pl.semaphore_wait(barrier, jnp.where(lat > 0, 4, 3))

    def remote(src, dst, send_sem, recv_sem, target):
        return pltpu.make_async_remote_copy(
            src_ref=src,
            dst_ref=dst,
            send_sem=send_sem,
            recv_sem=recv_sem,
            device_id=target,
            device_id_type=MESH,
        )

    to_east = remote(
        feat.at[:, breadth - EDGE : breadth], slab.at[0], slab_send.at[0], slab_recv.at[0], (lat, east)
    )
    to_west = remote(feat.at[:, 0:EDGE], slab.at[1], slab_send.at[1], slab_recv.at[1], (lat, west))
    to_east.start()
    to_west.start()
    rows_north = remote(
        feat.at[height - rim : height],
        rows.at[north_slot],
        rows_send.at[0],
        rows_recv.at[north_slot],
        north,
    )
    rows_south = remote(feat.at[0:rim], rows.at[1], rows_send.at[1], rows_recv.at[1], south)
    rows_north.start()

    @pl.when(lat > 0)
    def _():
        rows_south.start()

    row_id = lax.broadcasted_iota(jnp.int32, (ch, ch), 0)
    col_id = lax.broadcasted_iota(jnp.int32, (ch, ch), 1)
    diagonal = row_id == col_id
    nothing = jnp.zeros((ch, ch), BF16)
    for b in range(ks):
        for a in range(ks):
            block = jnp.where(diagonal, dw[a, b : b + 1, :], 0.0).astype(BF16)
            for o in range(2):
                i = (a + o) % 2
                d = (a + o - i) // 2
                base = ((d * ks + b) * 2 + i) * ch
                taps[base : base + ch, o * ch : (o + 1) * ch] = block
        base = ((0 * ks + b) * 2 + 0) * ch
        taps[base : base + ch, ch : 2 * ch] = nothing
        base = ((3 * ks + b) * 2 + 1) * ch
        taps[base : base + ch, 0:ch] = nothing

    def widen(r, carry):
        wide[r, FAR : FAR + breadth, :] = feat[r].astype(F32)
        return carry

    lax.fori_loop(0, height, widen, 0)

    to_east.wait_recv()
    to_west.wait_recv()

    corner_north = remote(
        slab.at[:, height - rim : height],
        corners.at[north_slot],
        corner_send.at[0],
        corner_recv.at[north_slot],
        north,
    )
    corner_south = remote(slab.at[:, 0:rim], corners.at[1], corner_send.at[1], corner_recv.at[1], south)
    corner_north.start()

    @pl.when(lat > 0)
    def _():
        corner_south.start()

    first = FAR - rim

    def spread_row(r, carry):
        wide[r, 0:FAR, :] = slab[0, r, EDGE - FAR : EDGE, :].astype(F32)
        wide[r, FAR + breadth :, :] = slab[1, r, 0:FAR, :].astype(F32)
        for o in range(n_off):
            ext[rim + r, o] = wide[r, pl.ds(first + o, blocks, stride=FAR), :].astype(BF16)
        return carry

    lax.fori_loop(0, height, spread_row, 0)

    turn = (
        lax.broadcasted_iota(jnp.int32, (blocks, blocks), 0)
        + lax.broadcasted_iota(jnp.int32, (blocks, blocks), 1)
        == blocks - 1
    ).astype(F32).astype(BF16)

    def ghost_tiles(slot, t):
        ghost_wide[t, FAR : FAR + breadth, :] = rows[slot, t].astype(F32)
        ghost_wide[t, 0:FAR, :] = corners[slot, 0, t, EDGE - FAR : EDGE, :].astype(F32)
        ghost_wide[t, FAR + breadth :, :] = corners[slot, 1, t, 0:FAR, :].astype(F32)
        return [
            ghost_wide[t, pl.ds(first + o, blocks, stride=FAR), :].astype(BF16) for o in range(n_off)
        ]

    def turned(tiles):
        flat = jnp.concatenate(tiles, axis=1)
        flat = jnp.dot(turn, flat, preferred_element_type=F32).astype(BF16)
        return [flat[:, o * ch : (o + 1) * ch] for o in range(len(tiles))][::-1]

    def ghost_rows():
        rows_north_in = remote(
            feat.at[0:rim], rows.at[1], rows_send.at[0], rows_recv.at[1], north
        )
        rows_north_in.wait_recv()
        remote(slab.at[:, 0:rim], corners.at[1], corner_send.at[0], corner_recv.at[1], north).wait_recv()

        @pl.when(top)
        def _():
            for t in range(rim):
                tiles = turned(ghost_tiles(1, rim - 1 - t))
                for o in range(n_off):
                    ext[rim + height + t, o] = tiles[o]

        @pl.when(jnp.logical_not(top))
        def _():
            for t in range(rim):
                tiles = ghost_tiles(1, t)
                for o in range(n_off):
                    ext[rim + height + t, o] = tiles[o]

        @pl.when(lat > 0)
        def _():
            remote(feat.at[0:rim], rows.at[0], rows_send.at[0], rows_recv.at[0], south).wait_recv()
            remote(
                slab.at[:, 0:rim], corners.at[0], corner_send.at[0], corner_recv.at[0], south
            ).wait_recv()
            for t in range(rim):
                tiles = ghost_tiles(0, t)
                for o in range(n_off):
                    ext[t, o] = tiles[o]

        @pl.when(lat == 0)
        def _():
            ext[0:rim] = jnp.zeros((rim, n_off, blocks, ch), BF16)

    def unit_at(step):
        inner = jnp.where(step < 2, step + 1, step - 1)
        return jnp.where(step == 2, 0, jnp.where(step == 3, units - 1, inner))

    def convolve(step):
        base = unit_at(step) * 4
        parts = []
        for pair in range(2):
            columns = []
            for d in range(4):
                for b in range(ks):
                    for i in range(2):
                        tile = ext[base + 2 * (pair + d) + i, b : b + FAR]
                        columns.append(tile.reshape(breadth, ch))
            parts.append(jnp.concatenate(columns, axis=1))
        lhs = jnp.concatenate(parts, axis=0)
        conv_out[lax.rem(step, 2)] = jnp.dot(lhs, taps[...], preferred_element_type=F32)

    order_row = lax.broadcasted_iota(jnp.int32, (breadth, breadth), 0)
    order_col = lax.broadcasted_iota(jnp.int32, (breadth, breadth), 1)
    placed = order_col == lax.rem(order_row, blocks) * FAR + order_row // blocks
    ones = jnp.ones((breadth, ch), BF16)

    def pointwise(step):
        base = unit_at(step) * 4
        for pair in range(2):
            part = conv_out[lax.rem(step, 2), pair * breadth : (pair + 1) * breadth, :]
            row = base + 2 * pair
            spatial = jnp.concatenate([part[:, 0:ch], part[:, ch : 2 * ch]], axis=0) + dw_bias[...]
            normed = layer_norm(spatial, gain1[...], shift1[...]).astype(BF16)
            hidden = []
            half = w1.shape[1] // 2
            for h in range(2):
                cut = slice(h * half, (h + 1) * half)
                lifted = jnp.dot(normed, w1[:, cut], preferred_element_type=F32) + b1[:, cut]
                hidden.append(gelu(lifted).astype(BF16))
            branch = jnp.dot(jnp.concatenate(hidden, axis=1), w2[...], preferred_element_type=F32)
            centre = jnp.concatenate(
                [ext[rim + row + i, rim : rim + FAR].reshape(breadth, ch) for i in range(2)], axis=0
            ).astype(F32)
            updated = centre + scale[...] * (branch + b2[...])
            picked = jnp.concatenate(
                [
                    jnp.where(placed, mask[pl.ds(row + i, 1), :].astype(F32), 0.0).astype(BF16)
                    for i in range(2)
                ],
                axis=0,
            )
            marks = jnp.dot(picked, ones, preferred_element_type=F32)
            normalized = marks * layer_norm(updated, gain2[...], shift2[...])
            for i in range(2):
                mine = normalized[i * breadth : (i + 1) * breadth]
                nrm[1 + row + i, 1 : 1 + FAR] = mine.astype(BF16).reshape(FAR, blocks, ch)
                at = lax.rem(step, 2) * 4 + 2 * pair + i
                side_out[0, step // 2, pl.ds(at, 1), :] = mine[breadth - 1 : breadth]
                side_out[1, step // 2, pl.ds(at, 1), :] = mine[0:1]

    def side_copy(way, pack):
        return remote(
            side_out.at[way, pack],
            side_in.at[way, pack],
            side_send.at[way, pack],
            side_recv.at[way, pack],
            (lat, east) if way == 0 else (lat, west),
        )

    def side_start(pack):
        for way in range(2):
            side_copy(way, pack).start()

    block_id = lax.broadcasted_iota(jnp.int32, (blocks, ch), 0)

    def side_finish(pack):
        for way in range(2):
            side_copy(way, pack).wait_recv()
        for part in range(2):
            base = unit_at(2 * pack + part) * 4
            for r in range(4):
                row = 1 + base + r
                at = part * 4 + r
                left = pltpu.roll(nrm[row, FAR].astype(F32), 1, 0)
                left = jnp.where(block_id == 0, side_in[0, pack, at : at + 1, :], left)
                nrm[row, 0] = left.astype(BF16)
                right = pltpu.roll(nrm[row, 1].astype(F32), blocks - 1, 0)
                right = jnp.where(block_id == blocks - 1, side_in[1, pack, at : at + 1, :], right)
                nrm[row, FAR + 1] = right.astype(BF16)

    stage_north = remote(
        nrm.at[height], stage.at[north_slot], stage_send.at[0], stage_recv.at[north_slot], north
    )
    stage_south = remote(nrm.at[1], stage.at[1], stage_send.at[1], stage_recv.at[1], south)

    def step_body(step, carry):
        @pl.when(step == 2)
        def _():
            ghost_rows()

        @pl.when(step == units - 2)
        def _():
            side_finish(1)
            stage_north.start()

            @pl.when(lat > 0)
            def _():
                stage_south.start()

        pointwise(step - 1)
        convolve(step)

        @pl.when(lax.rem(step, 2) == 0)
        def _():
            side_start(step // 2 - 1)

        return carry

    convolve(0)
    lax.fori_loop(1, units, step_body, 0)
    pointwise(units - 1)
    last = units // 2 - 1
    side_start(last)
    load_cw.wait()

    def shrink(first_row):
        parts = []
        for i in range(4):
            columns = []
            for a in range(4):
                for b in range(4):
                    tiles = [nrm[2 * (first_row + i) + a, 2 * o + b] for o in range(FAR // 2)]
                    columns.append(jnp.concatenate(tiles, axis=0))
            parts.append(jnp.concatenate(columns, axis=1))
        lhs = jnp.concatenate(parts, axis=0)
        total = jnp.dot(lhs, cw[...], preferred_element_type=F32) + cb[...]
        per_row = breadth // 2
        for i in range(4):
            for o in range(FAR // 2):
                at = i * per_row + o * blocks
                for h in range(total.shape[1] // 128):
                    lanes = slice(h * 128, (h + 1) * 128)
                    coarse[i, h, pl.ds(o, blocks, stride=FAR // 2), :] = total[at : at + blocks, lanes]
        for i in range(4):
            for h in range(total.shape[1] // 128):
                out[first_row + i, :, h * 128 : (h + 1) * 128] = coarse[i, h].astype(BF16)

    for pack in range(last):
        if pack != 1:
            side_finish(pack)

    remote(nrm.at[1], stage.at[1], stage_send.at[0], stage_recv.at[1], north).wait_recv()

    @pl.when(top)
    def _():
        tiles = turned([stage[1, o] for o in range(FAR + 2)])
        for o in range(FAR + 2):
            nrm[height + 1, o] = tiles[o]

    @pl.when(jnp.logical_not(top))
    def _():
        nrm[height + 1] = stage[1]

    @pl.when(lat > 0)
    def _():
        remote(nrm.at[1], stage.at[0], stage_send.at[0], stage_recv.at[0], south).wait_recv()
        nrm[0] = stage[0]

    @pl.when(lat == 0)
    def _():
        nrm[0] = jnp.zeros((FAR + 2, blocks, ch), BF16)

    groups = height // 8
    for g in range(groups):
        if g == groups - 2:
            side_finish(last)
        shrink(4 * g)

    to_east.wait_send()
    to_west.wait_send()
    rows_north.wait_send()
    corner_north.wait_send()
    stage_north.wait_send()
    for pack in range(units // 2):
        for way in range(2):
            side_copy(way, pack).wait_send()

    @pl.when(lat > 0)
    def _():
        rows_south.wait_send()
        corner_south.wait_send()
        stage_south.wait_send()


def local(
    features,
    land_mask,
    dw_weight,
    dw_bias,
    norm_gain,
    norm_shift,
    expand_weight,
    expand_bias,
    project_weight,
    project_bias,
    layer_scale,
    out_gain,
    out_shift,
    coarse_weight,
    coarse_bias,
):
    height, breadth, ch = features.shape
    ks = dw_weight.shape[0]
    rim = ks // 2
    blocks = breadth // FAR
    n_off = FAR + 2 * rim
    packs = height // 8
    outs = coarse_weight.shape[3]
    coarse_flat = coarse_weight.reshape(-1, outs)
    line = lambda v: v.reshape(1, -1)
    vmem = pl.BlockSpec(memory_space=pltpu.VMEM)
    dma = pltpu.SemaphoreType.DMA
    return pl.pallas_call(
        body,
        out_shape=jax.ShapeDtypeStruct((height // 2, breadth // 2, outs), BF16),
        in_specs=[vmem] * 13 + [pl.BlockSpec(memory_space=pl.ANY), vmem],
        out_specs=vmem,
        scratch_shapes=[
            pltpu.VMEM((2, height, EDGE, ch), BF16),
            pltpu.VMEM((2, rim, breadth, ch), BF16),
            pltpu.VMEM((2, 2, rim, EDGE, ch), BF16),
            pltpu.VMEM((height, breadth + 2 * FAR, ch), F32),
            pltpu.VMEM((rim, breadth + 2 * FAR, ch), F32),
            pltpu.VMEM((height + 2 * rim, n_off, blocks, ch), BF16),
            pltpu.VMEM((4 * ks * 2 * ch, 2 * ch), BF16),
            pltpu.VMEM((2, 2 * breadth, 2 * ch), F32),
            pltpu.VMEM((height + 2, FAR + 2, blocks, ch), BF16),
            pltpu.VMEM((2, packs, 8, ch), F32),
            pltpu.VMEM((2, packs, 8, ch), F32),
            pltpu.VMEM((2, FAR + 2, blocks, ch), BF16),
            pltpu.VMEM(coarse_flat.shape, BF16),
            pltpu.VMEM((4, outs // 128, breadth // 2, 128), F32),
            dma((2,)),
            dma((2,)),
            dma((2,)),
            dma((2,)),
            dma((2,)),
            dma((2,)),
            dma((2, packs)),
            dma((2, packs)),
            dma((2,)),
            dma((2,)),
            dma,
        ],
        compiler_params=pltpu.CompilerParams(
            collective_id=0, has_side_effects=True, vmem_limit_bytes=50 * 1024 * 1024
        ),
    )(
        features,
        land_mask,
        dw_weight,
        line(dw_bias),
        line(norm_gain),
        line(norm_shift),
        expand_weight,
        line(expand_bias),
        project_weight,
        line(project_bias),
        line(layer_scale),
        line(out_gain),
        line(out_shift),
        coarse_flat,
        line(coarse_bias),
    )


def solution(mesh):
    placed = (P("lat", "lon", None), P("lat", "lon")) + (P(),) * 13
    return jax.shard_map(
        local, mesh=mesh, in_specs=placed, out_specs=P("lat", "lon", None), check_vma=False
    )
```

```python
import jax
import jax.numpy as jnp
from jax import lax
from jax.experimental import pallas as pl
from jax.experimental.pallas import tpu as pltpu
from jax.sharding import PartitionSpec as P

MESH = pl.DeviceIdType.MESH
F32 = jnp.float32
BF16 = jnp.bfloat16
FAR = 8
EDGE = 16


ERF_FIT = (
    0.7978842854499817,
    0.03633416071534157,
    -3.303515768493526e-05,
    -5.5270647862926126e-05,
    3.973660568590276e-06,
    -1.337553072744413e-07,
    1.813239114412113e-09,
)
ERF_END = 27.04


def twice_gelu(values):
    square = jnp.minimum(values * values, ERF_END)
    slope = jnp.full_like(values, ERF_FIT[-1])
    for coefficient in ERF_FIT[-2::-1]:
        slope = slope * square + coefficient
    return values + values * jnp.tanh(values * slope)


def layer_norm(values, gain, shift):
    center = values - jnp.mean(values, axis=-1, keepdims=True)
    spread = jnp.mean(center * center, axis=-1, keepdims=True)
    return center * lax.rsqrt(spread + 1e-06) * gain + shift


def body(*refs):
    sources, out, held = refs[:15], refs[15], refs[16:31]
    (
        slab,
        rows,
        corners,
        wide,
        ghost_wide,
        ext,
        taps,
        conv_out,
        nrm,
        side_out,
        side_in,
        stage,
        coarse,
        slab_send,
        slab_recv,
        rows_send,
        rows_recv,
        corner_send,
        corner_recv,
        side_send,
        side_recv,
        stage_send,
        stage_recv,
        load_sem,
    ) = refs[31:]
    feat = sources[0]
    near = held[0]
    mask, dw, dw_bias, gain1, shift1, w1, b1, w2, b2, scale, gain2, shift2, cw, cb = held[1:]
    height, breadth, ch = feat.shape
    ks = dw.shape[0]
    rim = ks // 2
    blocks = breadth // FAR
    n_off = FAR + 2 * rim
    units = height // 4
    lat, lon = lax.axis_index("lat"), lax.axis_index("lon")
    n_lat, n_lon = lax.axis_size("lat"), lax.axis_size("lon")
    top = lat == n_lat - 1
    east, west = lax.rem(lon + 1, n_lon), lax.rem(lon + n_lon - 1, n_lon)
    north_lat = jnp.where(top, lat, lat + 1)
    north_lon = jnp.where(top, n_lon - 1 - lon, lon)
    north = (north_lat, north_lon)
    north_slot = jnp.where(top, 1, 0)
    south = (jnp.maximum(lat - 1, 0), lon)

    loads = [pltpu.make_async_copy(sources[k], held[k], load_sem.at[k]) for k in range(len(sources))]
    first_loads = (0, 2)
    for k in first_loads:
        loads[k].start()

    barrier = pltpu.get_barrier_semaphore()
    for target in ((lat, east), (lat, west), north):
        pl.semaphore_signal(barrier, inc=1, device_id=target, device_id_type=MESH)

    @pl.when(lat > 0)
    def _():
        pl.semaphore_signal(barrier, inc=1, device_id=south, device_id_type=MESH)

    pl.semaphore_wait(barrier, jnp.where(lat > 0, 4, 3))

    def remote(src, dst, send_sem, recv_sem, target):
        return pltpu.make_async_remote_copy(
            src_ref=src,
            dst_ref=dst,
            send_sem=send_sem,
            recv_sem=recv_sem,
            device_id=target,
            device_id_type=MESH,
        )

    to_east = remote(
        feat.at[:, breadth - EDGE : breadth], slab.at[0], slab_send.at[0], slab_recv.at[0], (lat, east)
    )
    to_west = remote(feat.at[:, 0:EDGE], slab.at[1], slab_send.at[1], slab_recv.at[1], (lat, west))
    to_east.start()
    to_west.start()
    rows_north = remote(
        feat.at[height - rim : height],
        rows.at[north_slot],
        rows_send.at[0],
        rows_recv.at[north_slot],
        north,
    )
    rows_south = remote(feat.at[0:rim], rows.at[1], rows_send.at[1], rows_recv.at[1], south)
    rows_north.start()

    @pl.when(lat > 0)
    def _():
        rows_south.start()

    for k in range(len(sources)):
        if k not in first_loads:
            loads[k].start()

    row_id = lax.broadcasted_iota(jnp.int32, (ch, ch), 0)
    col_id = lax.broadcasted_iota(jnp.int32, (ch, ch), 1)
    diagonal = row_id == col_id
    nothing = jnp.zeros((ch, ch), BF16)
    loads[2].wait()
    for b in range(ks):
        for a in range(ks):
            block = jnp.where(diagonal, dw[a, b : b + 1, :], 0.0).astype(BF16)
            for o in range(2):
                i = (a + o) % 2
                d = (a + o - i) // 2
                base = ((d * ks + b) * 2 + i) * ch
                taps[base : base + ch, o * ch : (o + 1) * ch] = block
        base = ((0 * ks + b) * 2 + 0) * ch
        taps[base : base + ch, ch : 2 * ch] = nothing
        base = ((3 * ks + b) * 2 + 1) * ch
        taps[base : base + ch, 0:ch] = nothing

    first = FAR - rim

    def pick(r, offsets):
        for o in offsets:
            ext[rim + r, o] = wide[r, pl.ds(first + o, blocks, stride=FAR), :].astype(BF16)

    def widen(k, carry):
        for r in range(4):
            wide[4 * k + r, FAR : FAR + breadth, :] = near[4 * k + r].astype(F32)
        for r in range(4):
            pick(4 * k + r, range(rim, rim + FAR))
        return carry

    loads[0].wait()
    lax.fori_loop(0, height // 4, widen, 0)

    to_east.wait_recv()
    to_west.wait_recv()

    corner_north = remote(
        slab.at[:, height - rim : height],
        corners.at[north_slot],
        corner_send.at[0],
        corner_recv.at[north_slot],
        north,
    )
    corner_south = remote(slab.at[:, 0:rim], corners.at[1], corner_send.at[1], corner_recv.at[1], south)
    corner_north.start()

    @pl.when(lat > 0)
    def _():
        corner_south.start()

    def widen_sides(k, carry):
        for r in range(4):
            wide[4 * k + r, 0:FAR, :] = slab[0, 4 * k + r, EDGE - FAR : EDGE, :].astype(F32)
            wide[4 * k + r, FAR + breadth :, :] = slab[1, 4 * k + r, 0:FAR, :].astype(F32)
        for r in range(4):
            pick(4 * k + r, (*range(rim), *range(rim + FAR, n_off)))
        return carry

    lax.fori_loop(0, height // 4, widen_sides, 0)

    turn = (
        lax.broadcasted_iota(jnp.int32, (blocks, blocks), 0)
        + lax.broadcasted_iota(jnp.int32, (blocks, blocks), 1)
        == blocks - 1
    ).astype(F32).astype(BF16)

    def ghost_tiles(slot, t):
        ghost_wide[t, FAR : FAR + breadth, :] = rows[slot, t].astype(F32)
        ghost_wide[t, 0:FAR, :] = corners[slot, 0, t, EDGE - FAR : EDGE, :].astype(F32)
        ghost_wide[t, FAR + breadth :, :] = corners[slot, 1, t, 0:FAR, :].astype(F32)
        return [
            ghost_wide[t, pl.ds(first + o, blocks, stride=FAR), :].astype(BF16) for o in range(n_off)
        ]

    def turned(tiles):
        flat = jnp.concatenate(tiles, axis=1)
        flat = jnp.dot(turn, flat, preferred_element_type=F32).astype(BF16)
        return [flat[:, o * ch : (o + 1) * ch] for o in range(len(tiles))][::-1]

    def ghost_rows():
        rows_north_in = remote(
            feat.at[0:rim], rows.at[1], rows_send.at[0], rows_recv.at[1], north
        )
        rows_north_in.wait_recv()
        remote(slab.at[:, 0:rim], corners.at[1], corner_send.at[0], corner_recv.at[1], north).wait_recv()

        @pl.when(top)
        def _():
            for t in range(rim):
                tiles = turned(ghost_tiles(1, rim - 1 - t))
                for o in range(n_off):
                    ext[rim + height + t, o] = tiles[o]

        @pl.when(jnp.logical_not(top))
        def _():
            for t in range(rim):
                tiles = ghost_tiles(1, t)
                for o in range(n_off):
                    ext[rim + height + t, o] = tiles[o]

        @pl.when(lat > 0)
        def _():
            remote(feat.at[0:rim], rows.at[0], rows_send.at[0], rows_recv.at[0], south).wait_recv()
            remote(
                slab.at[:, 0:rim], corners.at[0], corner_send.at[0], corner_recv.at[0], south
            ).wait_recv()
            for t in range(rim):
                tiles = ghost_tiles(0, t)
                for o in range(n_off):
                    ext[t, o] = tiles[o]

        @pl.when(lat == 0)
        def _():
            ext[0:rim] = jnp.zeros((rim, n_off, blocks, ch), BF16)

    def unit_at(step):
        inner = jnp.where(step < 2, step + 1, step - 1)
        return jnp.where(step == 2, 0, jnp.where(step == 3, units - 1, inner))

    def convolve(step):
        base = unit_at(step) * 4
        parts = []
        for pair in range(2):
            columns = []
            for d in range(4):
                for b in range(ks):
                    for i in range(2):
                        tile = ext[base + 2 * (pair + d) + i, b : b + FAR]
                        columns.append(tile.reshape(breadth, ch))
            parts.append(jnp.concatenate(columns, axis=1))
        lhs = jnp.concatenate(parts, axis=0)
        conv_out[lax.rem(step, 2)] = jnp.dot(lhs, taps[...], preferred_element_type=F32)

    order_row = lax.broadcasted_iota(jnp.int32, (breadth, breadth), 0)
    order_col = lax.broadcasted_iota(jnp.int32, (breadth, breadth), 1)
    placed = order_col == lax.rem(order_row, blocks) * FAR + order_row // blocks
    ones = jnp.ones((breadth, ch), BF16)

    def pointwise(step):
        base = unit_at(step) * 4
        for pair in range(2):
            part = conv_out[lax.rem(step, 2), pair * breadth : (pair + 1) * breadth, :]
            row = base + 2 * pair
            spatial = jnp.concatenate([part[:, 0:ch], part[:, ch : 2 * ch]], axis=0) + dw_bias[...]
            normed = layer_norm(spatial, gain1[...], shift1[...]).astype(BF16)
            hidden = []
            half = w1.shape[1] // 2
            for h in range(2):
                cut = slice(h * half, (h + 1) * half)
                lifted = jnp.dot(normed, w1[:, cut], preferred_element_type=F32) + b1[:, cut]
                hidden.append(twice_gelu(lifted).astype(BF16))
            branch = jnp.dot(jnp.concatenate(hidden, axis=1), w2[...], preferred_element_type=F32)
            centre = jnp.concatenate(
                [ext[rim + row + i, rim : rim + FAR].reshape(breadth, ch) for i in range(2)], axis=0
            ).astype(F32)
            updated = centre + scale[...] * (0.5 * branch + b2[...])
            picked = jnp.concatenate(
                [
                    jnp.where(placed, mask[pl.ds(row + i, 1), :].astype(F32), 0.0).astype(BF16)
                    for i in range(2)
                ],
                axis=0,
            )
            marks = jnp.dot(picked, ones, preferred_element_type=F32)
            normalized = marks * layer_norm(updated, gain2[...], shift2[...])
            for i in range(2):
                mine = normalized[i * breadth : (i + 1) * breadth]
                nrm[1 + row + i, 1 : 1 + FAR] = mine.astype(BF16).reshape(FAR, blocks, ch)
                at = lax.rem(step, 2) * 4 + 2 * pair + i
                side_out[0, step // 2, pl.ds(at, 1), :] = mine[breadth - 1 : breadth]
                side_out[1, step // 2, pl.ds(at, 1), :] = mine[0:1]

    def side_copy(way, pack):
        return remote(
            side_out.at[way, pack],
            side_in.at[way, pack],
            side_send.at[way, pack],
            side_recv.at[way, pack],
            (lat, east) if way == 0 else (lat, west),
        )

    def side_start(pack):
        for way in range(2):
            side_copy(way, pack).start()

    block_id = lax.broadcasted_iota(jnp.int32, (blocks, ch), 0)

    def side_finish(pack):
        for way in range(2):
            side_copy(way, pack).wait_recv()
        for part in range(2):
            base = unit_at(2 * pack + part) * 4
            for r in range(4):
                row = 1 + base + r
                at = part * 4 + r
                left = pltpu.roll(nrm[row, FAR].astype(F32), 1, 0)
                left = jnp.where(block_id == 0, side_in[0, pack, at : at + 1, :], left)
                nrm[row, 0] = left.astype(BF16)
                right = pltpu.roll(nrm[row, 1].astype(F32), blocks - 1, 0)
                right = jnp.where(block_id == blocks - 1, side_in[1, pack, at : at + 1, :], right)
                nrm[row, FAR + 1] = right.astype(BF16)

    stage_north = remote(
        nrm.at[height], stage.at[north_slot], stage_send.at[0], stage_recv.at[north_slot], north
    )
    stage_south = remote(nrm.at[1], stage.at[1], stage_send.at[1], stage_recv.at[1], south)

    def step_body(step, carry):
        @pl.when(step == 2)
        def _():
            ghost_rows()

        @pl.when(step == units - 2)
        def _():
            side_finish(1)
            stage_north.start()

            @pl.when(lat > 0)
            def _():
                stage_south.start()

        pointwise(step - 1)
        convolve(step)

        @pl.when(lax.rem(step, 2) == 0)
        def _():
            side_start(step // 2 - 1)

        return carry

    convolve(0)
    for k in range(len(sources)):
        if k not in first_loads and k < 13:
            loads[k].wait()
    lax.fori_loop(1, units, step_body, 0)
    pointwise(units - 1)
    last = units // 2 - 1
    side_start(last)
    loads[13].wait()
    loads[14].wait()

    def shrink(first_row):
        parts = []
        for i in range(4):
            columns = []
            for a in range(4):
                for b in range(4):
                    tiles = [nrm[2 * (first_row + i) + a, 2 * o + b] for o in range(FAR // 2)]
                    columns.append(jnp.concatenate(tiles, axis=0))
            parts.append(jnp.concatenate(columns, axis=1))
        lhs = jnp.concatenate(parts, axis=0)
        total = jnp.dot(lhs, cw[...], preferred_element_type=F32) + cb[...]
        per_row = breadth // 2
        for i in range(4):
            for o in range(FAR // 2):
                at = i * per_row + o * blocks
                for h in range(total.shape[1] // 128):
                    lanes = slice(h * 128, (h + 1) * 128)
                    coarse[i, h, pl.ds(o, blocks, stride=FAR // 2), :] = total[at : at + blocks, lanes]
        for i in range(4):
            for h in range(total.shape[1] // 128):
                out[first_row + i, :, h * 128 : (h + 1) * 128] = coarse[i, h].astype(BF16)

    for pack in range(last):
        if pack != 1:
            side_finish(pack)

    remote(nrm.at[1], stage.at[1], stage_send.at[0], stage_recv.at[1], north).wait_recv()

    @pl.when(top)
    def _():
        tiles = turned([stage[1, o] for o in range(FAR + 2)])
        for o in range(FAR + 2):
            nrm[height + 1, o] = tiles[o]

    @pl.when(jnp.logical_not(top))
    def _():
        nrm[height + 1] = stage[1]

    @pl.when(lat > 0)
    def _():
        remote(nrm.at[1], stage.at[0], stage_send.at[0], stage_recv.at[0], south).wait_recv()
        nrm[0] = stage[0]

    @pl.when(lat == 0)
    def _():
        nrm[0] = jnp.zeros((FAR + 2, blocks, ch), BF16)

    groups = height // 8
    for g in range(groups):
        if g == groups - 2:
            side_finish(last)
        shrink(4 * g)

    to_east.wait_send()
    to_west.wait_send()
    rows_north.wait_send()
    corner_north.wait_send()
    stage_north.wait_send()
    for pack in range(units // 2):
        for way in range(2):
            side_copy(way, pack).wait_send()

    @pl.when(lat > 0)
    def _():
        rows_south.wait_send()
        corner_south.wait_send()
        stage_south.wait_send()


def local(
    features,
    land_mask,
    dw_weight,
    dw_bias,
    norm_gain,
    norm_shift,
    expand_weight,
    expand_bias,
    project_weight,
    project_bias,
    layer_scale,
    out_gain,
    out_shift,
    coarse_weight,
    coarse_bias,
):
    height, breadth, ch = features.shape
    ks = dw_weight.shape[0]
    rim = ks // 2
    blocks = breadth // FAR
    n_off = FAR + 2 * rim
    packs = height // 8
    outs = coarse_weight.shape[3]
    coarse_flat = coarse_weight.reshape(-1, outs)
    line = lambda v: v.reshape(1, -1)
    anywhere = pl.BlockSpec(memory_space=pl.ANY)
    arrays = (
        features,
        land_mask,
        dw_weight,
        line(dw_bias),
        line(norm_gain),
        line(norm_shift),
        expand_weight,
        line(expand_bias),
        project_weight,
        line(project_bias),
        line(layer_scale),
        line(out_gain),
        line(out_shift),
        coarse_flat,
        line(coarse_bias),
    )
    dma = pltpu.SemaphoreType.DMA
    return pl.pallas_call(
        body,
        out_shape=jax.ShapeDtypeStruct((height // 2, breadth // 2, outs), BF16),
        in_specs=[anywhere] * len(arrays),
        out_specs=pl.BlockSpec(memory_space=pltpu.VMEM),
        scratch_shapes=[pltpu.VMEM(v.shape, v.dtype) for v in arrays]
        + [
            pltpu.VMEM((2, height, EDGE, ch), BF16),
            pltpu.VMEM((2, rim, breadth, ch), BF16),
            pltpu.VMEM((2, 2, rim, EDGE, ch), BF16),
            pltpu.VMEM((height, breadth + 2 * FAR, ch), F32),
            pltpu.VMEM((rim, breadth + 2 * FAR, ch), F32),
            pltpu.VMEM((height + 2 * rim, n_off, blocks, ch), BF16),
            pltpu.VMEM((4 * ks * 2 * ch, 2 * ch), BF16),
            pltpu.VMEM((2, 2 * breadth, 2 * ch), F32),
            pltpu.VMEM((height + 2, FAR + 2, blocks, ch), BF16),
            pltpu.VMEM((2, packs, 8, ch), F32),
            pltpu.VMEM((2, packs, 8, ch), F32),
            pltpu.VMEM((2, FAR + 2, blocks, ch), BF16),
            pltpu.VMEM((4, outs // 128, breadth // 2, 128), F32),
            dma((2,)),
            dma((2,)),
            dma((2,)),
            dma((2,)),
            dma((2,)),
            dma((2,)),
            dma((2, packs)),
            dma((2, packs)),
            dma((2,)),
            dma((2,)),
            dma((len(arrays),)),
        ],
        compiler_params=pltpu.CompilerParams(
            collective_id=0, has_side_effects=True, vmem_limit_bytes=56 * 1024 * 1024
        ),
    )(*arrays)


def solution(mesh):
    placed = (P("lat", "lon", None), P("lat", "lon")) + (P(),) * 13
    return jax.shard_map(
        local, mesh=mesh, in_specs=placed, out_specs=P("lat", "lon", None), check_vma=False
    )
```

```python
import functools

import jax
import jax.numpy as jnp
from jax import lax
from jax.experimental import pallas as pl
from jax.experimental.pallas import tpu as pltpu
from jax.sharding import PartitionSpec as P

MESH = pl.DeviceIdType.MESH
F32 = jnp.float32
BF16 = jnp.bfloat16
FAR = 8
EDGE = 16


ERF_FIT = (
    0.7978842854499817,
    0.03633416071534157,
    -3.303515768493526e-05,
    -5.5270647862926126e-05,
    3.973660568590276e-06,
    -1.337553072744413e-07,
    1.813239114412113e-09,
)
ERF_END = 27.04


def twice_gelu(values):
    square = jnp.minimum(values * values, ERF_END)
    slope = jnp.full_like(values, ERF_FIT[-1])
    for coefficient in ERF_FIT[-2::-1]:
        slope = slope * square + coefficient
    return values + values * jnp.tanh(values * slope)


def layer_norm(values, gain, shift):
    center = values - jnp.mean(values, axis=-1, keepdims=True)
    spread = jnp.mean(center * center, axis=-1, keepdims=True)
    return center * lax.rsqrt(spread + 1e-06) * gain + shift


def body(*refs):
    sources, out, held = refs[:15], refs[15], refs[16:31]
    (
        slab,
        rows,
        corners,
        wide,
        ghost_wide,
        ext,
        taps,
        conv_out,
        nrm,
        side_out,
        side_in,
        stage,
        coarse,
        slab_send,
        slab_recv,
        rows_send,
        rows_recv,
        corner_send,
        corner_recv,
        side_send,
        side_recv,
        stage_send,
        stage_recv,
        load_sem,
    ) = refs[31:]
    feat = sources[0]
    near = held[0]
    mask, dw, dw_bias, gain1, shift1, w1, b1, w2, b2, scale, gain2, shift2, cw, cb = held[1:]
    height, breadth, ch = feat.shape
    ks = dw.shape[0]
    rim = ks // 2
    blocks = breadth // FAR
    n_off = FAR + 2 * rim
    units = height // 4
    lat, lon = lax.axis_index("lat"), lax.axis_index("lon")
    n_lat, n_lon = lax.axis_size("lat"), lax.axis_size("lon")
    top = lat == n_lat - 1
    east, west = lax.rem(lon + 1, n_lon), lax.rem(lon + n_lon - 1, n_lon)
    north_lat = jnp.where(top, lat, lat + 1)
    north_lon = jnp.where(top, n_lon - 1 - lon, lon)
    north = (north_lat, north_lon)
    north_slot = jnp.where(top, 1, 0)
    south = (jnp.maximum(lat - 1, 0), lon)

    loads = [pltpu.make_async_copy(sources[k], held[k], load_sem.at[k]) for k in range(len(sources))]
    first_loads = (0, 2)
    for k in first_loads:
        loads[k].start()

    barrier = pltpu.get_barrier_semaphore()
    for target in ((lat, east), (lat, west), north):
        pl.semaphore_signal(barrier, inc=1, device_id=target, device_id_type=MESH)

    @pl.when(lat > 0)
    def _():
        pl.semaphore_signal(barrier, inc=1, device_id=south, device_id_type=MESH)

    pl.semaphore_wait(barrier, jnp.where(lat > 0, 4, 3))

    def remote(src, dst, send_sem, recv_sem, target):
        return pltpu.make_async_remote_copy(
            src_ref=src,
            dst_ref=dst,
            send_sem=send_sem,
            recv_sem=recv_sem,
            device_id=target,
            device_id_type=MESH,
        )

    to_east = remote(
        feat.at[:, breadth - EDGE : breadth], slab.at[0], slab_send.at[0], slab_recv.at[0], (lat, east)
    )
    to_west = remote(feat.at[:, 0:EDGE], slab.at[1], slab_send.at[1], slab_recv.at[1], (lat, west))
    to_east.start()
    to_west.start()
    rows_north = remote(
        feat.at[height - rim : height],
        rows.at[north_slot],
        rows_send.at[0],
        rows_recv.at[north_slot],
        north,
    )
    rows_south = remote(feat.at[0:rim], rows.at[1], rows_send.at[1], rows_recv.at[1], south)
    rows_north.start()

    @pl.when(lat > 0)
    def _():
        rows_south.start()

    for k in range(len(sources)):
        if k not in first_loads:
            loads[k].start()

    row_id = lax.broadcasted_iota(jnp.int32, (ch, ch), 0)
    col_id = lax.broadcasted_iota(jnp.int32, (ch, ch), 1)
    diagonal = row_id == col_id
    nothing = jnp.zeros((ch, ch), BF16)
    loads[2].wait()
    for b in range(ks):
        for a in range(ks):
            block = jnp.where(diagonal, dw[a, b : b + 1, :], 0.0).astype(BF16)
            for o in range(2):
                i = (a + o) % 2
                d = (a + o - i) // 2
                base = ((d * ks + b) * 2 + i) * ch
                taps[base : base + ch, o * ch : (o + 1) * ch] = block
        base = ((0 * ks + b) * 2 + 0) * ch
        taps[base : base + ch, ch : 2 * ch] = nothing
        base = ((3 * ks + b) * 2 + 1) * ch
        taps[base : base + ch, 0:ch] = nothing

    first = FAR - rim

    def pick(r, offsets):
        for o in offsets:
            ext[rim + r, o] = wide[r, pl.ds(first + o, blocks, stride=FAR), :].astype(BF16)

    def widen(k, carry):
        for r in range(4):
            wide[4 * k + r, FAR : FAR + breadth, :] = near[4 * k + r].astype(F32)
        for r in range(4):
            pick(4 * k + r, range(rim, rim + FAR))
        return carry

    loads[0].wait()
    lax.fori_loop(0, height // 4, widen, 0)

    to_east.wait_recv()
    to_west.wait_recv()

    corner_north = remote(
        slab.at[:, height - rim : height],
        corners.at[north_slot],
        corner_send.at[0],
        corner_recv.at[north_slot],
        north,
    )
    corner_south = remote(slab.at[:, 0:rim], corners.at[1], corner_send.at[1], corner_recv.at[1], south)
    corner_north.start()

    @pl.when(lat > 0)
    def _():
        corner_south.start()

    def widen_sides(k, carry):
        for r in range(4):
            wide[4 * k + r, 0:FAR, :] = slab[0, 4 * k + r, EDGE - FAR : EDGE, :].astype(F32)
            wide[4 * k + r, FAR + breadth :, :] = slab[1, 4 * k + r, 0:FAR, :].astype(F32)
        for r in range(4):
            pick(4 * k + r, (*range(rim), *range(rim + FAR, n_off)))
        return carry

    lax.fori_loop(0, height // 4, widen_sides, 0)

    turn = (
        lax.broadcasted_iota(jnp.int32, (blocks, blocks), 0)
        + lax.broadcasted_iota(jnp.int32, (blocks, blocks), 1)
        == blocks - 1
    ).astype(F32).astype(BF16)

    def ghost_tiles(slot, t):
        ghost_wide[t, FAR : FAR + breadth, :] = rows[slot, t].astype(F32)
        ghost_wide[t, 0:FAR, :] = corners[slot, 0, t, EDGE - FAR : EDGE, :].astype(F32)
        ghost_wide[t, FAR + breadth :, :] = corners[slot, 1, t, 0:FAR, :].astype(F32)
        return [
            ghost_wide[t, pl.ds(first + o, blocks, stride=FAR), :].astype(BF16) for o in range(n_off)
        ]

    def turned(tiles):
        flat = jnp.concatenate(tiles, axis=1)
        flat = jnp.dot(turn, flat, preferred_element_type=F32).astype(BF16)
        return [flat[:, o * ch : (o + 1) * ch] for o in range(len(tiles))][::-1]

    def ghost_rows():
        rows_north_in = remote(
            feat.at[0:rim], rows.at[1], rows_send.at[0], rows_recv.at[1], north
        )
        rows_north_in.wait_recv()
        remote(slab.at[:, 0:rim], corners.at[1], corner_send.at[0], corner_recv.at[1], north).wait_recv()

        @pl.when(top)
        def _():
            for t in range(rim):
                tiles = turned(ghost_tiles(1, rim - 1 - t))
                for o in range(n_off):
                    ext[rim + height + t, o] = tiles[o]

        @pl.when(jnp.logical_not(top))
        def _():
            for t in range(rim):
                tiles = ghost_tiles(1, t)
                for o in range(n_off):
                    ext[rim + height + t, o] = tiles[o]

        @pl.when(lat > 0)
        def _():
            remote(feat.at[0:rim], rows.at[0], rows_send.at[0], rows_recv.at[0], south).wait_recv()
            remote(
                slab.at[:, 0:rim], corners.at[0], corner_send.at[0], corner_recv.at[0], south
            ).wait_recv()
            for t in range(rim):
                tiles = ghost_tiles(0, t)
                for o in range(n_off):
                    ext[t, o] = tiles[o]

        @pl.when(lat == 0)
        def _():
            ext[0:rim] = jnp.zeros((rim, n_off, blocks, ch), BF16)

    def unit_at(step):
        inner = jnp.where(step < 2, step + 1, step - 1)
        return jnp.where(step == 2, 0, jnp.where(step == 3, units - 1, inner))

    def convolve(step, d):
        base = unit_at(step) * 4
        parts = []
        for pair in range(2):
            columns = []
            for b in range(ks):
                for i in range(2):
                    tile = ext[base + 2 * (pair + d) + i, b : b + FAR]
                    columns.append(tile.reshape(breadth, ch))
            parts.append(jnp.concatenate(columns, axis=1))
        lhs = jnp.concatenate(parts, axis=0)
        depth = 2 * ks * ch
        slot = lax.rem(step, 2)
        added = jnp.dot(lhs, taps[d * depth : (d + 1) * depth, :], preferred_element_type=F32)
        conv_out[slot] = added if d == 0 else conv_out[slot] + added

    order_row = lax.broadcasted_iota(jnp.int32, (breadth, breadth), 0)
    order_col = lax.broadcasted_iota(jnp.int32, (breadth, breadth), 1)
    placed = order_col == lax.rem(order_row, blocks) * FAR + order_row // blocks
    ones = jnp.ones((breadth, ch), BF16)

    def pointwise(step, between):
        base = unit_at(step) * 4
        slot = lax.rem(step, 2)
        half = w1.shape[1] // 2
        cuts = [slice(h * half, (h + 1) * half) for h in range(2)]

        def first_norm(pair):
            part = conv_out[slot, pair * breadth : (pair + 1) * breadth, :]
            spatial = jnp.concatenate([part[:, 0:ch], part[:, ch : 2 * ch]], axis=0) + dw_bias[...]
            return layer_norm(spatial, gain1[...], shift1[...]).astype(BF16)

        def lift(normed, cut):
            return jnp.dot(normed, w1[:, cut], preferred_element_type=F32) + b1[:, cut]

        def project(hidden):
            return jnp.dot(jnp.concatenate(hidden, axis=1), w2[...], preferred_element_type=F32)

        def spot(pair):
            row = base + 2 * pair
            picked = jnp.concatenate(
                [
                    jnp.where(placed, mask[pl.ds(row + i, 1), :].astype(F32), 0.0).astype(BF16)
                    for i in range(2)
                ],
                axis=0,
            )
            return jnp.dot(picked, ones, preferred_element_type=F32)

        def finish(pair, branch):
            row = base + 2 * pair
            centre = jnp.concatenate(
                [ext[rim + row + i, rim : rim + FAR].reshape(breadth, ch) for i in range(2)], axis=0
            ).astype(F32)
            updated = centre + scale[...] * (0.5 * branch + b2[...])
            normalized = spot(pair) * layer_norm(updated, gain2[...], shift2[...])
            for i in range(2):
                mine = normalized[i * breadth : (i + 1) * breadth]
                nrm[1 + row + i, 1 : 1 + FAR] = mine.astype(BF16).reshape(FAR, blocks, ch)
                at = slot * 4 + 2 * pair + i
                side_out[0, step // 2, pl.ds(at, 1), :] = mine[breadth - 1 : breadth]
                side_out[1, step // 2, pl.ds(at, 1), :] = mine[0:1]

        normed = [first_norm(pair) for pair in range(2)]
        work = [(pair, h) for pair in range(2) for h in range(2)]
        hidden = [[], []]
        lifted = lift(normed[0], cuts[0])
        for k, (pair, h) in enumerate(work):
            if k + 1 < len(work):
                coming = lift(normed[work[k + 1][0]], cuts[work[k + 1][1]])
            if between:
                between[k]()
            hidden[pair].append(twice_gelu(lifted).astype(BF16))
            if k + 1 < len(work):
                lifted = coming
            if k == 2:
                finish(0, project(hidden[0]))
        finish(1, project(hidden[1]))

    def side_copy(way, pack):
        return remote(
            side_out.at[way, pack],
            side_in.at[way, pack],
            side_send.at[way, pack],
            side_recv.at[way, pack],
            (lat, east) if way == 0 else (lat, west),
        )

    def side_start(pack):
        for way in range(2):
            side_copy(way, pack).start()

    block_id = lax.broadcasted_iota(jnp.int32, (blocks, ch), 0)

    def side_finish(pack):
        for way in range(2):
            side_copy(way, pack).wait_recv()
        for part in range(2):
            base = unit_at(2 * pack + part) * 4
            for r in range(4):
                row = 1 + base + r
                at = part * 4 + r
                left = pltpu.roll(nrm[row, FAR].astype(F32), 1, 0)
                left = jnp.where(block_id == 0, side_in[0, pack, at : at + 1, :], left)
                nrm[row, 0] = left.astype(BF16)
                right = pltpu.roll(nrm[row, 1].astype(F32), blocks - 1, 0)
                right = jnp.where(block_id == blocks - 1, side_in[1, pack, at : at + 1, :], right)
                nrm[row, FAR + 1] = right.astype(BF16)

    stage_north = remote(
        nrm.at[height], stage.at[north_slot], stage_send.at[0], stage_recv.at[north_slot], north
    )
    stage_south = remote(nrm.at[1], stage.at[1], stage_send.at[1], stage_recv.at[1], south)

    def step_body(step, carry):
        @pl.when(step == 2)
        def _():
            ghost_rows()

        @pl.when(step == units - 2)
        def _():
            side_finish(1)
            stage_north.start()

            @pl.when(lat > 0)
            def _():
                stage_south.start()

        pointwise(step - 1, [functools.partial(convolve, step, d) for d in range(4)])

        @pl.when(lax.rem(step, 2) == 0)
        def _():
            side_start(step // 2 - 1)

        return carry

    for d in range(4):
        convolve(0, d)
    for k in range(len(sources)):
        if k not in first_loads and k < 13:
            loads[k].wait()
    lax.fori_loop(1, units, step_body, 0)
    pointwise(units - 1, [])
    last = units // 2 - 1
    side_start(last)
    loads[13].wait()
    loads[14].wait()

    def shrink(first_row):
        parts = []
        for i in range(4):
            columns = []
            for a in range(4):
                for b in range(4):
                    tiles = [nrm[2 * (first_row + i) + a, 2 * o + b] for o in range(FAR // 2)]
                    columns.append(jnp.concatenate(tiles, axis=0))
            parts.append(jnp.concatenate(columns, axis=1))
        lhs = jnp.concatenate(parts, axis=0)
        total = jnp.dot(lhs, cw[...], preferred_element_type=F32) + cb[...]
        per_row = breadth // 2
        for i in range(4):
            for o in range(FAR // 2):
                at = i * per_row + o * blocks
                for h in range(total.shape[1] // 128):
                    lanes = slice(h * 128, (h + 1) * 128)
                    coarse[i, h, pl.ds(o, blocks, stride=FAR // 2), :] = total[at : at + blocks, lanes]
        for i in range(4):
            for h in range(total.shape[1] // 128):
                out[first_row + i, :, h * 128 : (h + 1) * 128] = coarse[i, h].astype(BF16)

    for pack in range(last):
        if pack != 1:
            side_finish(pack)

    remote(nrm.at[1], stage.at[1], stage_send.at[0], stage_recv.at[1], north).wait_recv()

    @pl.when(top)
    def _():
        tiles = turned([stage[1, o] for o in range(FAR + 2)])
        for o in range(FAR + 2):
            nrm[height + 1, o] = tiles[o]

    @pl.when(jnp.logical_not(top))
    def _():
        nrm[height + 1] = stage[1]

    @pl.when(lat > 0)
    def _():
        remote(nrm.at[1], stage.at[0], stage_send.at[0], stage_recv.at[0], south).wait_recv()
        nrm[0] = stage[0]

    @pl.when(lat == 0)
    def _():
        nrm[0] = jnp.zeros((FAR + 2, blocks, ch), BF16)

    groups = height // 8
    for g in range(groups):
        if g == groups - 2:
            side_finish(last)
        shrink(4 * g)

    to_east.wait_send()
    to_west.wait_send()
    rows_north.wait_send()
    corner_north.wait_send()
    stage_north.wait_send()
    for pack in range(units // 2):
        for way in range(2):
            side_copy(way, pack).wait_send()

    @pl.when(lat > 0)
    def _():
        rows_south.wait_send()
        corner_south.wait_send()
        stage_south.wait_send()


def local(
    features,
    land_mask,
    dw_weight,
    dw_bias,
    norm_gain,
    norm_shift,
    expand_weight,
    expand_bias,
    project_weight,
    project_bias,
    layer_scale,
    out_gain,
    out_shift,
    coarse_weight,
    coarse_bias,
):
    height, breadth, ch = features.shape
    ks = dw_weight.shape[0]
    rim = ks // 2
    blocks = breadth // FAR
    n_off = FAR + 2 * rim
    packs = height // 8
    outs = coarse_weight.shape[3]
    coarse_flat = coarse_weight.reshape(-1, outs)
    line = lambda v: v.reshape(1, -1)
    anywhere = pl.BlockSpec(memory_space=pltpu.HBM)
    arrays = (
        features,
        land_mask,
        dw_weight,
        line(dw_bias),
        line(norm_gain),
        line(norm_shift),
        expand_weight,
        line(expand_bias),
        project_weight,
        line(project_bias),
        line(layer_scale),
        line(out_gain),
        line(out_shift),
        coarse_flat,
        line(coarse_bias),
    )
    dma = pltpu.SemaphoreType.DMA
    return pl.pallas_call(
        body,
        out_shape=jax.ShapeDtypeStruct((height // 2, breadth // 2, outs), BF16),
        in_specs=[anywhere] * len(arrays),
        out_specs=pl.BlockSpec(memory_space=pltpu.VMEM),
        scratch_shapes=[pltpu.VMEM(v.shape, v.dtype) for v in arrays]
        + [
            pltpu.VMEM((2, height, EDGE, ch), BF16),
            pltpu.VMEM((2, rim, breadth, ch), BF16),
            pltpu.VMEM((2, 2, rim, EDGE, ch), BF16),
            pltpu.VMEM((height, breadth + 2 * FAR, ch), F32),
            pltpu.VMEM((rim, breadth + 2 * FAR, ch), F32),
            pltpu.VMEM((height + 2 * rim, n_off, blocks, ch), BF16),
            pltpu.VMEM((4 * ks * 2 * ch, 2 * ch), BF16),
            pltpu.VMEM((2, 2 * breadth, 2 * ch), F32),
            pltpu.VMEM((height + 2, FAR + 2, blocks, ch), BF16),
            pltpu.VMEM((2, packs, 8, ch), F32),
            pltpu.VMEM((2, packs, 8, ch), F32),
            pltpu.VMEM((2, FAR + 2, blocks, ch), BF16),
            pltpu.VMEM((4, outs // 128, breadth // 2, 128), F32),
            dma((2,)),
            dma((2,)),
            dma((2,)),
            dma((2,)),
            dma((2,)),
            dma((2,)),
            dma((2, packs)),
            dma((2, packs)),
            dma((2,)),
            dma((2,)),
            dma((len(arrays),)),
        ],
        compiler_params=pltpu.CompilerParams(
            collective_id=0, has_side_effects=True, vmem_limit_bytes=40 * 1024 * 1024
        ),
    )(*arrays)


def solution(mesh):
    placed = (P("lat", "lon", None), P("lat", "lon")) + (P(),) * 13
    return jax.shard_map(
        local, mesh=mesh, in_specs=placed, out_specs=P("lat", "lon", None), check_vma=False
    )
```

```python
import functools

import jax
import jax.numpy as jnp
from jax import lax
from jax.experimental import pallas as pl
from jax.experimental.pallas import tpu as pltpu
from jax.sharding import PartitionSpec as P

MESH = pl.DeviceIdType.MESH
F32 = jnp.float32
BF16 = jnp.bfloat16
FAR = 8
EDGE = 16


ERF_FIT = (
    0.7978842854499817,
    0.03633416071534157,
    -3.303515768493526e-05,
    -5.5270647862926126e-05,
    3.973660568590276e-06,
    -1.337553072744413e-07,
    1.813239114412113e-09,
)
ERF_END = 27.04


def twice_gelu(values):
    square = jnp.minimum(values * values, ERF_END)
    slope = jnp.full_like(values, ERF_FIT[-1])
    for coefficient in ERF_FIT[-2::-1]:
        slope = slope * square + coefficient
    return values + values * jnp.tanh(values * slope)


def layer_norm(values, gain, shift):
    center = values - jnp.mean(values, axis=-1, keepdims=True)
    spread = jnp.mean(center * center, axis=-1, keepdims=True)
    return center * lax.rsqrt(spread + 1e-06) * gain + shift


def body(*refs):
    sources, out, held = refs[:15], refs[15], refs[16:31]
    (
        slab,
        rows,
        corners,
        wide,
        ghost_wide,
        ext,
        taps,
        conv_out,
        nrm,
        side_out,
        side_in,
        stage,
        coarse,
        slab_send,
        slab_recv,
        rows_send,
        rows_recv,
        corner_send,
        corner_recv,
        side_send,
        side_recv,
        stage_send,
        stage_recv,
        load_sem,
    ) = refs[31:]
    feat = sources[0]
    near = held[0]
    mask, dw, dw_bias, gain1, shift1, w1, b1, w2, b2, scale, gain2, shift2, cw, cb = held[1:]
    height, breadth, ch = feat.shape
    ks = dw.shape[0]
    rim = ks // 2
    blocks = breadth // FAR
    n_off = FAR + 2 * rim
    units = height // 4
    lat, lon = lax.axis_index("lat"), lax.axis_index("lon")
    n_lat, n_lon = lax.axis_size("lat"), lax.axis_size("lon")
    top = lat == n_lat - 1
    east, west = lax.rem(lon + 1, n_lon), lax.rem(lon + n_lon - 1, n_lon)
    north_lat = jnp.where(top, lat, lat + 1)
    north_lon = jnp.where(top, n_lon - 1 - lon, lon)
    north = (north_lat, north_lon)
    north_slot = jnp.where(top, 1, 0)
    south = (jnp.maximum(lat - 1, 0), lon)

    loads = [pltpu.make_async_copy(sources[k], held[k], load_sem.at[k]) for k in range(len(sources))]
    first_loads = (0, 2)
    for k in first_loads:
        loads[k].start()

    barrier = pltpu.get_barrier_semaphore()
    for target in ((lat, east), (lat, west), north):
        pl.semaphore_signal(barrier, inc=1, device_id=target, device_id_type=MESH)

    @pl.when(lat > 0)
    def _():
        pl.semaphore_signal(barrier, inc=1, device_id=south, device_id_type=MESH)

    pl.semaphore_wait(barrier, jnp.where(lat > 0, 4, 3))

    def remote(src, dst, send_sem, recv_sem, target):
        return pltpu.make_async_remote_copy(
            src_ref=src,
            dst_ref=dst,
            send_sem=send_sem,
            recv_sem=recv_sem,
            device_id=target,
            device_id_type=MESH,
        )

    to_east = remote(
        feat.at[:, breadth - EDGE : breadth], slab.at[0], slab_send.at[0], slab_recv.at[0], (lat, east)
    )
    to_west = remote(feat.at[:, 0:EDGE], slab.at[1], slab_send.at[1], slab_recv.at[1], (lat, west))
    to_east.start()
    to_west.start()
    rows_north = remote(
        feat.at[height - rim : height],
        rows.at[north_slot],
        rows_send.at[0],
        rows_recv.at[north_slot],
        north,
    )
    rows_south = remote(feat.at[0:rim], rows.at[1], rows_send.at[1], rows_recv.at[1], south)
    rows_north.start()

    @pl.when(lat > 0)
    def _():
        rows_south.start()

    for k in range(len(sources)):
        if k not in first_loads:
            loads[k].start()

    row_id = lax.broadcasted_iota(jnp.int32, (ch, ch), 0)
    col_id = lax.broadcasted_iota(jnp.int32, (ch, ch), 1)
    diagonal = row_id == col_id
    nothing = jnp.zeros((ch, ch), BF16)
    loads[2].wait()
    for b in range(ks):
        for a in range(ks):
            block = jnp.where(diagonal, dw[a, b : b + 1, :], 0.0).astype(BF16)
            for o in range(2):
                i = (a + o) % 2
                d = (a + o - i) // 2
                base = ((d * ks + b) * 2 + i) * ch
                taps[base : base + ch, o * ch : (o + 1) * ch] = block
        base = ((0 * ks + b) * 2 + 0) * ch
        taps[base : base + ch, ch : 2 * ch] = nothing
        base = ((3 * ks + b) * 2 + 1) * ch
        taps[base : base + ch, 0:ch] = nothing

    first = FAR - rim

    def pick(r, offsets):
        for o in offsets:
            ext[rim + r, o] = wide[r, pl.ds(first + o, blocks, stride=FAR), :].astype(BF16)

    def widen(k, carry):
        for r in range(4):
            wide[4 * k + r, FAR : FAR + breadth, :] = near[4 * k + r].astype(F32)
        for r in range(4):
            pick(4 * k + r, range(rim, rim + FAR))
        return carry

    loads[0].wait()
    lax.fori_loop(0, height // 4, widen, 0)

    to_east.wait_recv()
    to_west.wait_recv()

    corner_north = remote(
        slab.at[:, height - rim : height],
        corners.at[north_slot],
        corner_send.at[0],
        corner_recv.at[north_slot],
        north,
    )
    corner_south = remote(slab.at[:, 0:rim], corners.at[1], corner_send.at[1], corner_recv.at[1], south)
    corner_north.start()

    @pl.when(lat > 0)
    def _():
        corner_south.start()

    def widen_sides(k, carry):
        for r in range(4):
            wide[4 * k + r, 0:FAR, :] = slab[0, 4 * k + r, EDGE - FAR : EDGE, :].astype(F32)
            wide[4 * k + r, FAR + breadth :, :] = slab[1, 4 * k + r, 0:FAR, :].astype(F32)
        for r in range(4):
            pick(4 * k + r, (*range(rim), *range(rim + FAR, n_off)))
        return carry

    lax.fori_loop(0, height // 4, widen_sides, 0)

    turn = (
        lax.broadcasted_iota(jnp.int32, (blocks, blocks), 0)
        + lax.broadcasted_iota(jnp.int32, (blocks, blocks), 1)
        == blocks - 1
    ).astype(F32).astype(BF16)

    def ghost_tiles(slot, t):
        ghost_wide[t, FAR : FAR + breadth, :] = rows[slot, t].astype(F32)
        ghost_wide[t, 0:FAR, :] = corners[slot, 0, t, EDGE - FAR : EDGE, :].astype(F32)
        ghost_wide[t, FAR + breadth :, :] = corners[slot, 1, t, 0:FAR, :].astype(F32)
        return [
            ghost_wide[t, pl.ds(first + o, blocks, stride=FAR), :].astype(BF16) for o in range(n_off)
        ]

    def turned(tiles):
        flat = jnp.concatenate(tiles, axis=1)
        flat = jnp.dot(turn, flat, preferred_element_type=F32).astype(BF16)
        return [flat[:, o * ch : (o + 1) * ch] for o in range(len(tiles))][::-1]

    def ghost_rows():
        rows_north_in = remote(
            feat.at[0:rim], rows.at[1], rows_send.at[0], rows_recv.at[1], north
        )
        rows_north_in.wait_recv()
        remote(slab.at[:, 0:rim], corners.at[1], corner_send.at[0], corner_recv.at[1], north).wait_recv()

        @pl.when(top)
        def _():
            for t in range(rim):
                tiles = turned(ghost_tiles(1, rim - 1 - t))
                for o in range(n_off):
                    ext[rim + height + t, o] = tiles[o]

        @pl.when(jnp.logical_not(top))
        def _():
            for t in range(rim):
                tiles = ghost_tiles(1, t)
                for o in range(n_off):
                    ext[rim + height + t, o] = tiles[o]

        @pl.when(lat > 0)
        def _():
            remote(feat.at[0:rim], rows.at[0], rows_send.at[0], rows_recv.at[0], south).wait_recv()
            remote(
                slab.at[:, 0:rim], corners.at[0], corner_send.at[0], corner_recv.at[0], south
            ).wait_recv()
            for t in range(rim):
                tiles = ghost_tiles(0, t)
                for o in range(n_off):
                    ext[t, o] = tiles[o]

        @pl.when(lat == 0)
        def _():
            ext[0:rim] = jnp.zeros((rim, n_off, blocks, ch), BF16)

    def unit_at(step):
        inner = jnp.where(step < 2, step + 1, step - 1)
        return jnp.where(step == 2, 0, jnp.where(step == 3, units - 1, inner))

    def convolve(pack, d):
        parts = []
        for part in range(2):
            base = unit_at(2 * pack + part) * 4
            for pair in range(2):
                columns = []
                for b in range(ks):
                    for i in range(2):
                        tile = ext[base + 2 * (pair + d) + i, b : b + FAR]
                        columns.append(tile.reshape(breadth, ch))
                parts.append(jnp.concatenate(columns, axis=1))
        lhs = jnp.concatenate(parts, axis=0)
        depth = 2 * ks * ch
        slot = lax.rem(pack, 2)
        added = jnp.dot(lhs, taps[d * depth : (d + 1) * depth, :], preferred_element_type=F32)
        conv_out[slot] = added if d == 0 else conv_out[slot] + added

    order_row = lax.broadcasted_iota(jnp.int32, (breadth, breadth), 0)
    order_col = lax.broadcasted_iota(jnp.int32, (breadth, breadth), 1)
    placed = order_col == lax.rem(order_row, blocks) * FAR + order_row // blocks
    ones = jnp.ones((breadth, ch), BF16)

    def pointwise(pack, part_id, between):
        base = unit_at(2 * pack + part_id) * 4
        slot = lax.rem(pack, 2)
        half = w1.shape[1] // 2
        cuts = [slice(h * half, (h + 1) * half) for h in range(2)]

        def first_norm(pair):
            begin = (2 * part_id + pair) * breadth
            part = conv_out[slot, begin : begin + breadth, :]
            spatial = jnp.concatenate([part[:, 0:ch], part[:, ch : 2 * ch]], axis=0) + dw_bias[...]
            return layer_norm(spatial, gain1[...], shift1[...]).astype(BF16)

        def lift(normed, cut):
            return jnp.dot(normed, w1[:, cut], preferred_element_type=F32) + b1[:, cut]

        def project(hidden):
            return jnp.dot(jnp.concatenate(hidden, axis=1), w2[...], preferred_element_type=F32)

        def spot(pair):
            row = base + 2 * pair
            picked = jnp.concatenate(
                [
                    jnp.where(placed, mask[pl.ds(row + i, 1), :].astype(F32), 0.0).astype(BF16)
                    for i in range(2)
                ],
                axis=0,
            )
            return jnp.dot(picked, ones, preferred_element_type=F32)

        def finish(pair, branch):
            row = base + 2 * pair
            centre = jnp.concatenate(
                [ext[rim + row + i, rim : rim + FAR].reshape(breadth, ch) for i in range(2)], axis=0
            ).astype(F32)
            updated = centre + scale[...] * (0.5 * branch + b2[...])
            normalized = spot(pair) * layer_norm(updated, gain2[...], shift2[...])
            for i in range(2):
                mine = normalized[i * breadth : (i + 1) * breadth]
                nrm[1 + row + i, 1 : 1 + FAR] = mine.astype(BF16).reshape(FAR, blocks, ch)
                at = part_id * 4 + 2 * pair + i
                side_out[0, pack, at : at + 1, :] = mine[breadth - 1 : breadth]
                side_out[1, pack, at : at + 1, :] = mine[0:1]

        normed = [first_norm(pair) for pair in range(2)]
        work = [(pair, h) for pair in range(2) for h in range(2)]
        hidden = [[], []]
        lifted = lift(normed[0], cuts[0])
        for k, (pair, h) in enumerate(work):
            if k + 1 < len(work):
                coming = lift(normed[work[k + 1][0]], cuts[work[k + 1][1]])
            if k % 2 == 0 and between:
                between[k // 2]()
            hidden[pair].append(twice_gelu(lifted).astype(BF16))
            if k + 1 < len(work):
                lifted = coming
            if k == 2:
                finish(0, project(hidden[0]))
        finish(1, project(hidden[1]))

    def side_copy(way, pack):
        return remote(
            side_out.at[way, pack],
            side_in.at[way, pack],
            side_send.at[way, pack],
            side_recv.at[way, pack],
            (lat, east) if way == 0 else (lat, west),
        )

    def side_start(pack):
        for way in range(2):
            side_copy(way, pack).start()

    block_id = lax.broadcasted_iota(jnp.int32, (blocks, ch), 0)

    def side_finish(pack):
        for way in range(2):
            side_copy(way, pack).wait_recv()
        for part in range(2):
            base = unit_at(2 * pack + part) * 4
            for r in range(4):
                row = 1 + base + r
                at = part * 4 + r
                left = pltpu.roll(nrm[row, FAR].astype(F32), 1, 0)
                left = jnp.where(block_id == 0, side_in[0, pack, at : at + 1, :], left)
                nrm[row, 0] = left.astype(BF16)
                right = pltpu.roll(nrm[row, 1].astype(F32), blocks - 1, 0)
                right = jnp.where(block_id == blocks - 1, side_in[1, pack, at : at + 1, :], right)
                nrm[row, FAR + 1] = right.astype(BF16)

    stage_north = remote(
        nrm.at[height], stage.at[north_slot], stage_send.at[0], stage_recv.at[north_slot], north
    )
    stage_south = remote(nrm.at[1], stage.at[1], stage_send.at[1], stage_recv.at[1], south)

    last = units // 2 - 1

    def pack_body(pack, carry):
        @pl.when(pack == 1)
        def _():
            ghost_rows()

        @pl.when(pack == last)
        def _():
            side_finish(1)
            stage_north.start()

            @pl.when(lat > 0)
            def _():
                stage_south.start()

        for part in range(2):
            pieces = [functools.partial(convolve, pack, 2 * part + d) for d in range(2)]
            pointwise(pack - 1, part, pieces)
        side_start(pack - 1)
        return carry

    for d in range(4):
        convolve(0, d)
    for k in range(len(sources)):
        if k not in first_loads and k < 13:
            loads[k].wait()
    lax.fori_loop(1, last + 1, pack_body, 0)
    for part in range(2):
        pointwise(last, part, [])
    side_start(last)
    loads[13].wait()
    loads[14].wait()

    def shrink(first_row):
        parts = []
        for i in range(4):
            columns = []
            for a in range(4):
                for b in range(4):
                    tiles = [nrm[2 * (first_row + i) + a, 2 * o + b] for o in range(FAR // 2)]
                    columns.append(jnp.concatenate(tiles, axis=0))
            parts.append(jnp.concatenate(columns, axis=1))
        lhs = jnp.concatenate(parts, axis=0)
        total = jnp.dot(lhs, cw[...], preferred_element_type=F32) + cb[...]
        per_row = breadth // 2
        for i in range(4):
            for o in range(FAR // 2):
                at = i * per_row + o * blocks
                for h in range(total.shape[1] // 128):
                    lanes = slice(h * 128, (h + 1) * 128)
                    coarse[i, h, pl.ds(o, blocks, stride=FAR // 2), :] = total[at : at + blocks, lanes]
        for i in range(4):
            for h in range(total.shape[1] // 128):
                out[first_row + i, :, h * 128 : (h + 1) * 128] = coarse[i, h].astype(BF16)

    for pack in range(last):
        if pack != 1:
            side_finish(pack)

    remote(nrm.at[1], stage.at[1], stage_send.at[0], stage_recv.at[1], north).wait_recv()

    @pl.when(top)
    def _():
        tiles = turned([stage[1, o] for o in range(FAR + 2)])
        for o in range(FAR + 2):
            nrm[height + 1, o] = tiles[o]

    @pl.when(jnp.logical_not(top))
    def _():
        nrm[height + 1] = stage[1]

    @pl.when(lat > 0)
    def _():
        remote(nrm.at[1], stage.at[0], stage_send.at[0], stage_recv.at[0], south).wait_recv()
        nrm[0] = stage[0]

    @pl.when(lat == 0)
    def _():
        nrm[0] = jnp.zeros((FAR + 2, blocks, ch), BF16)

    groups = height // 8
    for g in range(groups):
        if g == groups - 2:
            side_finish(last)
        shrink(4 * g)

    to_east.wait_send()
    to_west.wait_send()
    rows_north.wait_send()
    corner_north.wait_send()
    stage_north.wait_send()
    for pack in range(units // 2):
        for way in range(2):
            side_copy(way, pack).wait_send()

    @pl.when(lat > 0)
    def _():
        rows_south.wait_send()
        corner_south.wait_send()
        stage_south.wait_send()


def local(
    features,
    land_mask,
    dw_weight,
    dw_bias,
    norm_gain,
    norm_shift,
    expand_weight,
    expand_bias,
    project_weight,
    project_bias,
    layer_scale,
    out_gain,
    out_shift,
    coarse_weight,
    coarse_bias,
):
    height, breadth, ch = features.shape
    ks = dw_weight.shape[0]
    rim = ks // 2
    blocks = breadth // FAR
    n_off = FAR + 2 * rim
    packs = height // 8
    outs = coarse_weight.shape[3]
    coarse_flat = coarse_weight.reshape(-1, outs)
    line = lambda v: v.reshape(1, -1)
    anywhere = pl.BlockSpec(memory_space=pltpu.HBM)
    arrays = (
        features,
        land_mask,
        dw_weight,
        line(dw_bias),
        line(norm_gain),
        line(norm_shift),
        expand_weight,
        line(expand_bias),
        project_weight,
        line(project_bias),
        line(layer_scale),
        line(out_gain),
        line(out_shift),
        coarse_flat,
        line(coarse_bias),
    )
    dma = pltpu.SemaphoreType.DMA
    return pl.pallas_call(
        body,
        out_shape=jax.ShapeDtypeStruct((height // 2, breadth // 2, outs), BF16),
        in_specs=[anywhere] * len(arrays),
        out_specs=pl.BlockSpec(memory_space=pltpu.VMEM),
        scratch_shapes=[pltpu.VMEM(v.shape, v.dtype) for v in arrays]
        + [
            pltpu.VMEM((2, height, EDGE, ch), BF16),
            pltpu.VMEM((2, rim, breadth, ch), BF16),
            pltpu.VMEM((2, 2, rim, EDGE, ch), BF16),
            pltpu.VMEM((height, breadth + 2 * FAR, ch), F32),
            pltpu.VMEM((rim, breadth + 2 * FAR, ch), F32),
            pltpu.VMEM((height + 2 * rim, n_off, blocks, ch), BF16),
            pltpu.VMEM((4 * ks * 2 * ch, 2 * ch), BF16),
            pltpu.VMEM((2, 4 * breadth, 2 * ch), F32),
            pltpu.VMEM((height + 2, FAR + 2, blocks, ch), BF16),
            pltpu.VMEM((2, packs, 8, ch), F32),
            pltpu.VMEM((2, packs, 8, ch), F32),
            pltpu.VMEM((2, FAR + 2, blocks, ch), BF16),
            pltpu.VMEM((4, outs // 128, breadth // 2, 128), F32),
            dma((2,)),
            dma((2,)),
            dma((2,)),
            dma((2,)),
            dma((2,)),
            dma((2,)),
            dma((2, packs)),
            dma((2, packs)),
            dma((2,)),
            dma((2,)),
            dma((len(arrays),)),
        ],
        compiler_params=pltpu.CompilerParams(
            collective_id=0, has_side_effects=True, vmem_limit_bytes=56 * 1024 * 1024
        ),
    )(*arrays)


def solution(mesh):
    placed = (P("lat", "lon", None), P("lat", "lon")) + (P(),) * 13
    return jax.shard_map(
        local, mesh=mesh, in_specs=placed, out_specs=P("lat", "lon", None), check_vma=False
    )
```
